32 devices in a mesh: blk: 16 (over z, y, core), group: 2 (over x).
Axes of the slice: x: 2, y: 2, z: 4, core: 2. Of those that a mesh axis runs over, the one named last changes fastest.
Arguments:
- audio_embed: float32 [12288, 512], P('blk'), may hold values from -4 to 4
- text_embed: float32 [12288, 512], P(('blk', 'group')), may hold values from -4 to 4
Outputs:
- grad_audio: float32 [12288, 512], P(('blk', 'group'))
- grad_text: float32 [12288, 512], P(('blk', 'group'))
- loss_rows: float32 [12288], P(('blk', 'group'))
- loss_cols: float32 [12288], P(('blk', 'group'))
The draws below stay inside these ranges and needn't reach their ends.
All inputs are finite; a program needn't handle non-finite values.
Results may differ from the reference program's by a relative error of at most 0.0003.
Values sent between devices are 32-bit elements; how exact they have to be, the bound alone decides.
A program may use at most 64 MiB of HBM per device.

```python
import jax
import jax.numpy as jnp
from jax import lax

D = 512
RB = 768
SPAN = 3
PAIRS = 12288
N_BLK = 16


def joint_draw(key):
    subkeys = jax.random.split(jax.random.fold_in(key, 11), 2)
    audio_noise = jax.random.normal(subkeys[0], (PAIRS, D), jnp.float32)
    text_noise = jax.random.normal(subkeys[1], (PAIRS, D), jnp.float32)
    audio_out = 0.1 * audio_noise
    text_out = 0.1 * text_noise
    return (jnp.clip(audio_out, -4.0, 4.0), jnp.clip(text_out, -4.0, 4.0))


def draw_audio_embed(key, part):
    return joint_draw(key)[0]


def draw_text_embed(key, part):
    return joint_draw(key)[1]


def setup_inputs(seed: int = 0) -> dict:
    seeds = jax.random.split(jax.random.key(seed), 3)
    return {
        "audio_embed": draw_audio_embed(jax.random.fold_in(seeds[2], 71), 0),
        "text_embed": draw_text_embed(jax.random.fold_in(seeds[2], 71), 0),
    }


logit_scale = 1.0 / 0.07
precise = lax.Precision.HIGHEST


def window_blocks(blocks, block):
    picked = ((block + jnp.arange(SPAN, dtype=jnp.int32)) % N_BLK).astype(jnp.int32)
    return jnp.take(blocks, picked, axis=0)


def scores(audio_block, window):
    return logit_scale * jnp.einsum("rd,kcd->rkc", audio_block, window, precision=precise)


def reference(audio_embed, text_embed):
    text_blocks = text_embed.reshape(N_BLK, RB, D)
    audio_blocks = audio_embed.reshape(N_BLK, RB, D)
    indices = jnp.arange(N_BLK, dtype=jnp.int32)

    def forward(block):
        audio_block = lax.dynamic_index_in_dim(audio_blocks, block, 0, keepdims=False)
        logits = scores(audio_block, window_blocks(text_blocks, block))
        row_top = jnp.max(logits, axis=(1, 2))
        row_lse = row_top + jnp.log(jnp.sum(jnp.exp(logits - row_top[:, None, None]), axis=(1, 2)))
        col_top = jnp.max(logits, axis=0)
        col_sum = jnp.sum(jnp.exp(logits - col_top[None]), axis=0)
        return row_lse, col_top, col_sum

    row_lse, col_top, col_sum = lax.map(forward, indices)
    tile_maxima = jnp.stack([jnp.roll(col_top[:, offset], offset, axis=0) for offset in range(SPAN)])
    tile_sums = jnp.stack([jnp.roll(col_sum[:, offset], offset, axis=0) for offset in range(SPAN)])
    highest = jnp.max(tile_maxima, axis=0)
    col_lse = highest + jnp.log(jnp.sum(tile_sums * jnp.exp(tile_maxima - highest[None]), axis=0))
    positive = jnp.eye(RB, dtype=jnp.float32)[:, None, :] * (jnp.arange(SPAN) == 0).astype(jnp.float32)[None, :, None]

    def backward(block):
        audio_block = lax.dynamic_index_in_dim(audio_blocks, block, 0, keepdims=False)
        window = window_blocks(text_blocks, block)
        logits = scores(audio_block, window)
        lse_window = window_blocks(col_lse, block)
        row_block = lax.dynamic_index_in_dim(row_lse, block, 0, keepdims=False)
        soft_weights = 0.5 * (jnp.exp(logits - row_block[:, None, None]) + jnp.exp(logits - lse_window[None]))
        grad_logits = soft_weights - positive
        audio_part = logit_scale * jnp.einsum("rkc,kcd->rd", grad_logits, window, precision=precise)
        text_parts = logit_scale * jnp.einsum("rkc,rd->kcd", grad_logits, audio_block, precision=precise)
        positive_scores = jnp.diagonal(logits[:, 0, :])
        return audio_part, text_parts, row_block - positive_scores, positive_scores

    audio_parts, text_parts, loss_rows, positive_scores = lax.map(backward, indices)
    grad_text = text_parts[:, 0]
    for offset in range(1, SPAN):
        grad_text = grad_text + jnp.roll(text_parts[:, offset], offset, axis=0)
    loss_cols = col_lse - positive_scores
    return (audio_parts.reshape(PAIRS, D), grad_text.reshape(PAIRS, D), loss_rows.reshape(PAIRS), loss_cols.reshape(PAIRS))
```

```python
import functools
import math

import jax
import jax.numpy as jnp
from jax import lax
from jax.experimental import pallas as pl
from jax.experimental.pallas import tpu as pltpu
from jax.sharding import PartitionSpec as P

SPAN = 3
LANES = 128
MESH = pl.DeviceIdType.MESH

logit_scale = 1.0 / 0.07
log2e = math.log2(math.e)
ln2 = math.log(2.0)
bf16 = jnp.bfloat16
f32 = jnp.float32


def split(value):
    high = value.astype(bf16)
    return high, (value - high.astype(f32)).astype(bf16)


def dot(a, b):
    return jnp.dot(a, b, preferred_element_type=f32)


def dot3(a_high, a_low, b_high, b_low):
    return dot(a_high, b_high) + dot(a_high, b_low) + dot(a_low, b_high)


def merge(first, second):
    highest = jnp.maximum(first[0], second[0])
    return (
        highest,
        first[1] * jnp.exp2(first[0] - highest) + second[1] * jnp.exp2(second[0] - highest),
    )


def kernel(
    n_blk, n_group, parts,
    audio, text,
    grad_audio, grad_text, loss_rows, loss_cols,
    window, audio_high, audio_low, turned_high, turned_low,
    text_turned_high, text_turned_low, logits, g_high, g_low,
    audio_part, audio_inbox,
    text_part, inbox, relay,
    tall, wide, col_box, row_box, row_stat,
    fwd_send, fwd_recv, stat_send, stat_recv, row_send, row_recv,
    back_send, back_recv, ga_send, ga_recv,
):
    rows, depth = audio.shape
    cols = text.shape[0]
    chunk = cols // parts
    padded = wide.shape[2]
    b = lax.axis_index("blk")
    member = lax.axis_index("group")
    odd = lax.rem(b, 2) == 1
    even = lax.rem(b, 2) == 0

    def at(step, group=None):
        return {
            "blk": lax.rem(b + step + n_blk, n_blk),
            "group": member if group is None else group,
        }

    def peer(step):
        return lax.rem(member + step, n_group)

    barrier = pltpu.get_barrier_semaphore()
    for step in (-2, -1, 1, 2):
        pl.semaphore_signal(barrier, inc=1, device_id=at(step), device_id_type=MESH)
    for step in range(1, n_group):
        pl.semaphore_signal(barrier, inc=1, device_id=at(0, peer(step)), device_id_type=MESH)
    pl.semaphore_wait(barrier, 4 + n_group - 1)

    def piece(c):
        return pl.ds(c * chunk, chunk)

    def remote(src, dst, send, recv, device):
        return pltpu.make_async_remote_copy(
            src_ref=src, dst_ref=dst, send_sem=send, recv_sem=recv,
            device_id=device, device_id_type=MESH,
        )

    def near(c):
        return remote(text.at[piece(c)], window.at[0, piece(c)], fwd_send.at[0, c], fwd_recv.at[0, c], at(-1))

    def far(c):
        return remote(text.at[piece(c)], window.at[1, piece(c)], fwd_send.at[1, c], fwd_recv.at[1, c], at(-2))

    def pass_on(c):
        return remote(
            window.at[0, piece(c)], window.at[1, piece(c)], fwd_send.at[2, c], fwd_recv.at[1, c], at(-1)
        )

    for c in range(parts):
        near(c).start()
    for c in range(parts):
        @pl.when(odd)
        def _():
            far(c).start()

    scaled = audio[...] * (logit_scale * log2e)
    high, low = split(scaled)
    audio_high[...] = high
    audio_low[...] = low
    turned = scaled.T
    high, low = split(turned)
    turned_high[...] = high
    turned_low[...] = low
    tall[...] = jnp.zeros_like(tall)
    row_stat[...] = jnp.zeros_like(row_stat)

    ids_text = lax.broadcasted_iota(jnp.int32, (chunk, rows), 0)
    ids_audio = lax.broadcasted_iota(jnp.int32, (chunk, rows), 1)

    def positive(c):
        return ids_audio == ids_text + (member * cols + c * chunk)

    lane = lax.broadcasted_iota(jnp.int32, (chunk, LANES), 1)

    def stat_copy(mine, theirs):
        return remote(
            wide.at[mine], col_box.at[theirs, mine],
            stat_send.at[theirs, mine], stat_recv.at[theirs, mine], at(mine - theirs),
        )

    for k in range(SPAN):
        for c in range(parts):
            if k == 0:
                block = text[piece(c)]
            else:
                if k == 1:
                    near(c).wait_recv()

                    @pl.when(odd)
                    def _():
                        pass_on(c).start()
                else:
                    far(c).wait_recv()
                block = window[k - 1, piece(c)]
            high, low = split(block)
            start = k * cols + c * chunk
            tile = dot3(high, low, turned_high[...], turned_low[...])
            logits[pl.ds(start, chunk)] = tile
            top = jnp.max(tile, axis=1, keepdims=True)
            total = jnp.sum(jnp.exp2(tile - top), axis=1, keepdims=True)
            tall[piece(c)] = jnp.where(lane == 0, top, total)
            top = jnp.max(tile, axis=0, keepdims=True)
            if start:
                top = jnp.maximum(top, row_stat[0:1])
            total = jnp.sum(jnp.exp2(tile - top), axis=0, keepdims=True)
            if start:
                total = total + row_stat[1:2] * jnp.exp2(row_stat[0:1] - top)
            row_stat[0:1] = top
            row_stat[1:2] = total
        wide[k] = tall[...].T[0:8]
        for theirs in range(SPAN):
            if theirs != k:
                stat_copy(k, theirs).start()
        if k == SPAN - 1:
            for step in range(1, n_group):
                remote(
                    row_stat, row_box.at[step], row_send.at[step], row_recv.at[step], at(0, peer(step))
                ).start()
        block = text[...] if k == 0 else window[k - 1]
        high, low = split(block.T)
        text_turned_high[k] = high
        text_turned_low[k] = low

    pair = (row_stat[0:1], row_stat[1:2])
    for step in range(1, n_group):
        remote(
            row_stat, row_box.at[step], row_send.at[step], row_recv.at[step], at(0, peer(step))
        ).wait_recv()
        pair = merge(pair, (row_box[step, 0:1], row_box[step, 1:2]))
    row_lse = pair[0] + jnp.log2(pair[1])

    def back(k, c):
        part = text_part.at[k, piece(c)]
        if k == 2:
            return (
                remote(part, inbox.at[1, piece(c)], back_send.at[1, c], back_recv.at[1, c], at(2)),
                remote(part, relay.at[piece(c)], back_send.at[1, c], back_recv.at[2, c], at(1)),
            )
        return remote(part, inbox.at[0, piece(c)], back_send.at[0, c], back_recv.at[0, c], at(1))

    def weights(k):
        pair = (wide[k, 0:1], wide[k, 1:2])
        for other in range(SPAN):
            if other != k:
                stat_copy(other, k).wait_recv()
                pair = merge(pair, (col_box[k, other, 0:1], col_box[k, other, 1:2]))
        col_lse = jnp.broadcast_to(pair[0] + jnp.log2(pair[1]), (LANES, padded)).T
        for c in range(parts):
            start = k * cols + c * chunk
            tile = logits[pl.ds(start, chunk)]
            own_lse = col_lse[c * chunk:(c + 1) * chunk, 0:1]
            weight = 0.5 * (jnp.exp2(tile - row_lse) + jnp.exp2(tile - own_lse))
            if k == 0:
                here = positive(c)
                weight = jnp.where(here, weight - 1.0, weight)
                score = jnp.sum(jnp.where(here, tile, 0.0), axis=1, keepdims=True)
                own_row = jnp.sum(jnp.where(here, row_lse, 0.0), axis=1, keepdims=True)
                tall[piece(c)] = ln2 * jnp.where(lane == 0, own_row - score, own_lse - score)
            high, low = split(weight)
            g_high[pl.ds(start, chunk)] = high
            g_low[pl.ds(start, chunk)] = low

    def text_terms(k, c):
        here = pl.ds(k * cols + c * chunk, chunk)
        return ln2 * dot3(g_high[here], g_low[here], audio_high[...], audio_low[...])

    weights(2)
    for c in range(parts):
        text_part[2, piece(c)] = text_terms(2, c)

        @pl.when(odd)
        def _():
            back(2, c)[0].start()

        @pl.when(even)
        def _():
            back(2, c)[1].start()

    weights(1)
    for c in range(parts):
        text_part[1, piece(c)] = text_terms(1, c)

        @pl.when(odd)
        def _():
            back(2, c)[1].wait_recv()
            text_part[1, piece(c)] += relay[piece(c)]

        back(1, c).start()

    weights(0)
    losses = tall[...].T
    loss_rows[...] = losses[0:1, 0:cols]
    loss_cols[...] = losses[1:2, 0:cols]

    span = 256 if rows % 256 == 0 else rows
    for start in range(0, rows, span):
        total = None
        for k in range(SPAN):
            here = (pl.ds(k * cols, cols), pl.ds(start, span))
            term = dot3(text_turned_high[k], text_turned_low[k], g_high[here], g_low[here])
            total = term if total is None else total + term
        audio_part[pl.ds(start, span)] = logit_scale * total.T

    def share(group):
        return pl.ds(pl.multiple_of(group * cols, 8), cols)

    def spread(step):
        return remote(
            audio_part.at[share(peer(step))], audio_inbox.at[step],
            ga_send.at[step], ga_recv.at[step], at(0, peer(step)),
        )

    for step in range(1, n_group):
        spread(step).start()

    for c in range(parts):
        text_part[0, piece(c)] = text_terms(0, c)

    total = audio_part[share(member)]
    for step in range(1, n_group):
        spread(step).wait_recv()
        total = total + audio_inbox[step]
    grad_audio[...] = total

    for c in range(parts):
        back(1, c).wait_recv()
        grad_text[piece(c)] = text_part[0, piece(c)] + inbox[0, piece(c)]

        @pl.when(odd)
        def _():
            back(2, c)[0].wait_recv()
            grad_text[piece(c)] += inbox[1, piece(c)]

    for c in range(parts):
        near(c).wait_send()
        back(2, c)[0].wait_send()
        back(1, c).wait_send()

        @pl.when(odd)
        def _():
            far(c).wait_send()
            pass_on(c).wait_send()

    for mine in range(SPAN):
        for theirs in range(SPAN):
            if mine != theirs:
                stat_copy(mine, theirs).wait_send()
    for step in range(1, n_group):
        remote(
            row_stat, row_box.at[step], row_send.at[step], row_recv.at[step], at(0, peer(step))
        ).wait_send()
        spread(step).wait_send()


def shards(n_blk, n_group, audio_embed, text_embed):
    rows, depth = audio_embed.shape
    cols = text_embed.shape[0]
    parts = 2
    padded = -(-cols // LANES) * LANES
    vmem = pl.BlockSpec(memory_space=pltpu.VMEM)
    dma = pltpu.SemaphoreType.DMA
    grad_audio, grad_text, loss_rows, loss_cols = pl.pallas_call(
        functools.partial(kernel, n_blk, n_group, parts),
        out_shape=(
            jax.ShapeDtypeStruct((cols, depth), f32),
            jax.ShapeDtypeStruct((cols, depth), f32),
            jax.ShapeDtypeStruct((1, cols), f32),
            jax.ShapeDtypeStruct((1, cols), f32),
        ),
        in_specs=[vmem, vmem],
        out_specs=(vmem, vmem, vmem, vmem),
        scratch_shapes=[
            pltpu.VMEM((SPAN - 1, cols, depth), f32),
            pltpu.VMEM((rows, depth), bf16),
            pltpu.VMEM((rows, depth), bf16),
            pltpu.VMEM((depth, rows), bf16),
            pltpu.VMEM((depth, rows), bf16),
            pltpu.VMEM((SPAN, depth, cols), bf16),
            pltpu.VMEM((SPAN, depth, cols), bf16),
            pltpu.VMEM((SPAN * cols, rows), f32),
            pltpu.VMEM((SPAN * cols, rows), bf16),
            pltpu.VMEM((SPAN * cols, rows), bf16),
            pltpu.VMEM((rows, depth), f32),
            pltpu.VMEM((n_group, cols, depth), f32),
            pltpu.VMEM((SPAN, cols, depth), f32),
            pltpu.VMEM((2, cols, depth), f32),
            pltpu.VMEM((cols, depth), f32),
            pltpu.VMEM((padded, LANES), f32),
            pltpu.VMEM((SPAN, 8, padded), f32),
            pltpu.VMEM((SPAN, SPAN, 8, padded), f32),
            pltpu.VMEM((n_group, 8, rows), f32),
            pltpu.VMEM((8, rows), f32),
            dma((3, parts)), dma((2, parts)),
            dma((SPAN, SPAN)), dma((SPAN, SPAN)),
            dma((n_group,)), dma((n_group,)),
            dma((2, parts)), dma((3, parts)),
            dma((n_group,)), dma((n_group,)),
        ],
        compiler_params=pltpu.CompilerParams(
            collective_id=0, has_side_effects=True, vmem_limit_bytes=56 * 1024 * 1024
        ),
        name="contrast",
    )(audio_embed, text_embed)
    return grad_audio, grad_text, loss_rows.reshape(cols), loss_cols.reshape(cols)


def solution(mesh):
    return jax.shard_map(
        functools.partial(shards, mesh.shape["blk"], mesh.shape["group"]),
        mesh=mesh,
        in_specs=(P("blk", None), P(("blk", "group"), None)),
        out_specs=(
            P(("blk", "group"), None),
            P(("blk", "group"), None),
            P(("blk", "group")),
            P(("blk", "group")),
        ),
        check_vma=False,
    )
```

```python
import functools
import math

import jax
import jax.numpy as jnp
from jax import lax
from jax.experimental import pallas as pl
from jax.experimental.pallas import tpu as pltpu
from jax.sharding import PartitionSpec as P

SPAN = 3
LANES = 128
MESH = pl.DeviceIdType.MESH

logit_scale = 1.0 / 0.07
log2e = math.log2(math.e)
ln2 = math.log(2.0)
bf16 = jnp.bfloat16
f32 = jnp.float32


def split(value):
    high = value.astype(bf16)
    return high, (value - high.astype(f32)).astype(bf16)


def dot(a, b):
    return jnp.dot(a, b, preferred_element_type=f32)


def dot3(a_high, a_low, b_high, b_low):
    return dot(a_high, b_high) + dot(a_high, b_low) + dot(a_low, b_high)


def merge(first, second):
    highest = jnp.maximum(first[0], second[0])
    return (
        highest,
        first[1] * jnp.exp2(first[0] - highest) + second[1] * jnp.exp2(second[0] - highest),
    )


def kernel(
    n_blk, n_group, parts, steps,
    audio, text,
    grad_audio, grad_text, loss_rows, loss_cols,
    window, audio_high, audio_low, turned_high, turned_low,
    text_turned_high, text_turned_low, logits, g_high, g_low,
    audio_part, audio_inbox,
    text_part, inbox, relay,
    tall, wide, col_box, row_box, row_stat,
    fwd_send, fwd_recv, stat_send, stat_recv, row_send, row_recv,
    back_send, back_recv, ga_send, ga_recv,
):
    rows, depth = audio.shape
    cols = text.shape[0]
    chunk = cols // parts
    strip = cols // steps
    padded = wide.shape[2]
    b = lax.axis_index("blk")
    member = lax.axis_index("group")
    odd = lax.rem(b, 2) == 1
    even = lax.rem(b, 2) == 0

    def at(step, group=None):
        return {
            "blk": lax.rem(b + step + n_blk, n_blk),
            "group": member if group is None else group,
        }

    def peer(step):
        return lax.rem(member + step, n_group)

    barrier = pltpu.get_barrier_semaphore()
    for step in (-2, -1, 1, 2):
        pl.semaphore_signal(barrier, inc=1, device_id=at(step), device_id_type=MESH)
    for step in range(1, n_group):
        pl.semaphore_signal(barrier, inc=1, device_id=at(0, peer(step)), device_id_type=MESH)
    pl.semaphore_wait(barrier, 4 + n_group - 1)

    def piece(c):
        return pl.ds(c * chunk, chunk)

    def remote(src, dst, send, recv, device):
        return pltpu.make_async_remote_copy(
            src_ref=src, dst_ref=dst, send_sem=send, recv_sem=recv,
            device_id=device, device_id_type=MESH,
        )

    def near(c):
        return remote(text.at[piece(c)], window.at[0, piece(c)], fwd_send.at[0, c], fwd_recv.at[0, c], at(-1))

    def far(c):
        return remote(text.at[piece(c)], window.at[1, piece(c)], fwd_send.at[1, c], fwd_recv.at[1, c], at(-2))

    def pass_on(c):
        return remote(
            window.at[0, piece(c)], window.at[1, piece(c)], fwd_send.at[2, c], fwd_recv.at[1, c], at(-1)
        )

    for c in range(parts):
        near(c).start()
    scaled = audio[...] * (logit_scale * log2e)
    high, low = split(scaled)
    audio_high[...] = high
    audio_low[...] = low
    turned = scaled.T
    high, low = split(turned)
    turned_high[...] = high
    turned_low[...] = low
    tall[...] = jnp.zeros_like(tall)
    row_stat[...] = jnp.zeros_like(row_stat)

    def positive(c):
        ids_text = lax.broadcasted_iota(jnp.int32, (strip, rows), 0)
        ids_audio = lax.broadcasted_iota(jnp.int32, (strip, rows), 1)
        return ids_audio == ids_text + (member * cols + c * strip)

    lane = lax.broadcasted_iota(jnp.int32, (chunk, LANES), 1)

    def stat_copy(mine, theirs):
        return remote(
            wide.at[mine], col_box.at[theirs, mine],
            stat_send.at[theirs, mine], stat_recv.at[theirs, mine], at(mine - theirs),
        )

    for k in range(SPAN):
        if k == 1:
            @pl.when(odd)
            def _():
                far(0).start()

        for c in range(parts):
            if k == 0:
                block = text[piece(c)]
            else:
                if k == 1:
                    near(c).wait_recv()

                    @pl.when(odd)
                    def _():
                        pass_on(c).start()
                        if c + 1 < parts:
                            far(c + 1).start()
                else:
                    far(c).wait_recv()
                block = window[k - 1, piece(c)]
            high, low = split(block)
            start = k * cols + c * chunk
            tile = dot3(high, low, turned_high[...], turned_low[...])
            logits[pl.ds(start, chunk)] = tile
            top = jnp.max(tile, axis=1, keepdims=True)
            total = jnp.sum(jnp.exp2(tile - top), axis=1, keepdims=True)
            tall[piece(c)] = jnp.where(lane == 0, top, total)
            top = jnp.max(tile, axis=0, keepdims=True)
            if start:
                top = jnp.maximum(top, row_stat[0:1])
            total = jnp.sum(jnp.exp2(tile - top), axis=0, keepdims=True)
            if start:
                total = total + row_stat[1:2] * jnp.exp2(row_stat[0:1] - top)
            row_stat[0:1] = top
            row_stat[1:2] = total
        wide[k] = tall[...].T[0:8]
        for theirs in range(SPAN):
            if theirs != k:
                stat_copy(k, theirs).start()
        if k == SPAN - 1:
            for step in range(1, n_group):
                remote(
                    row_stat, row_box.at[step], row_send.at[step], row_recv.at[step], at(0, peer(step))
                ).start()
        block = text[...] if k == 0 else window[k - 1]
        high, low = split(block.T)
        text_turned_high[k] = high
        text_turned_low[k] = low

    pair = (row_stat[0:1], row_stat[1:2])
    for step in range(1, n_group):
        remote(
            row_stat, row_box.at[step], row_send.at[step], row_recv.at[step], at(0, peer(step))
        ).wait_recv()
        pair = merge(pair, (row_box[step, 0:1], row_box[step, 1:2]))
    row_lse = pair[0] + jnp.log2(pair[1])

    def stripe(c):
        return pl.ds(c * strip, strip)

    def back(k, c, onward=True):
        part = text_part.at[k, stripe(c)]
        if k == 2 and onward:
            return remote(part, inbox.at[1, stripe(c)], back_send.at[1, c], back_recv.at[1, c], at(2))
        if k == 2:
            return remote(part, relay.at[stripe(c)], back_send.at[1, c], back_recv.at[2, c], at(1))
        return remote(part, inbox.at[0, stripe(c)], back_send.at[0, c], back_recv.at[0, c], at(1))

    def column_lse(k):
        pair = (wide[k, 0:1], wide[k, 1:2])
        for other in range(SPAN):
            if other != k:
                stat_copy(other, k).wait_recv()
                pair = merge(pair, (col_box[k, other, 0:1], col_box[k, other, 1:2]))
        return jnp.broadcast_to(pair[0] + jnp.log2(pair[1]), (LANES, padded)).T

    def weights(k, c, col_lse):
        start = k * cols + c * strip
        tile = logits[pl.ds(start, strip)]
        own_lse = col_lse[c * strip:(c + 1) * strip, 0:1]
        weight = 0.5 * (jnp.exp2(tile - row_lse) + jnp.exp2(tile - own_lse))
        if k == 0:
            here = positive(c)
            weight = jnp.where(here, weight - 1.0, weight)
            score = jnp.sum(jnp.where(here, tile, 0.0), axis=1, keepdims=True)
            own_row = jnp.sum(jnp.where(here, row_lse, 0.0), axis=1, keepdims=True)
            lanes = lax.broadcasted_iota(jnp.int32, (strip, LANES), 1)
            tall[stripe(c)] = jnp.where(lanes == 0, own_row - score, own_lse - score)
        high, low = split(weight)
        g_high[pl.ds(start, strip)] = high
        g_low[pl.ds(start, strip)] = low

    def text_terms(k, c):
        here = pl.ds(k * cols + c * strip, strip)
        return dot3(g_high[here], g_low[here], audio_high[...], audio_low[...])

    col_lse = column_lse(2)
    for c in range(steps):
        weights(2, c, col_lse)
        text_part[2, stripe(c)] = text_terms(2, c)

        @pl.when(odd)
        def _():
            back(2, c).start()

        @pl.when(even)
        def _():
            back(2, c, False).start()

    for k in (1, 0):
        col_lse = column_lse(k)
        for c in range(steps):
            weights(k, c, col_lse)

    def audio_terms(lanes):
        total = None
        for k in range(SPAN):
            here = (pl.ds(k * cols, cols), lanes)
            term = dot3(text_turned_high[k], text_turned_low[k], g_high[here], g_low[here])
            total = term if total is None else total + term
        return total.T

    def share(group):
        return pl.ds(pl.multiple_of(group * cols, 8), cols)

    def spread(step):
        return remote(
            audio_part.at[share(peer(step))], audio_inbox.at[step],
            ga_send.at[step], ga_recv.at[step], at(0, peer(step)),
        )

    aligned = cols % LANES == 0

    def own_share(step):
        start = peer(step) * cols
        audio_part[share(peer(step))] = audio_terms(pl.ds(pl.multiple_of(start, LANES), cols))

    if not aligned:
        audio_part[...] = audio_terms(pl.ds(0, rows))
    for step in range(1, n_group):
        if aligned:
            own_share(step)
        spread(step).start()

    for c in range(steps):
        text_part[1, stripe(c)] = text_terms(1, c)

        @pl.when(odd)
        def _():
            back(2, c, False).wait_recv()
            text_part[1, stripe(c)] += relay[stripe(c)]

        back(1, c).start()

    losses = tall[...].T
    loss_rows[...] = losses[0:1, 0:cols].reshape(loss_rows.shape)
    loss_cols[...] = losses[1:2, 0:cols].reshape(loss_cols.shape)

    for c in range(steps):
        text_part[0, stripe(c)] = text_terms(0, c)
    if aligned:
        own_share(0)

    total = audio_part[share(member)]
    for step in range(1, n_group):
        spread(step).wait_recv()
        total = total + audio_inbox[step]
    grad_audio[...] = total

    for c in range(steps):
        back(1, c).wait_recv()
        grad_text[stripe(c)] = text_part[0, stripe(c)] + inbox[0, stripe(c)]

        @pl.when(odd)
        def _():
            back(2, c).wait_recv()
            grad_text[stripe(c)] += inbox[1, stripe(c)]

    for c in range(steps):
        back(2, c).wait_send()
        back(1, c).wait_send()

    for c in range(parts):
        near(c).wait_send()

        @pl.when(odd)
        def _():
            far(c).wait_send()
            pass_on(c).wait_send()

    for mine in range(SPAN):
        for theirs in range(SPAN):
            if mine != theirs:
                stat_copy(mine, theirs).wait_send()
    for step in range(1, n_group):
        remote(
            row_stat, row_box.at[step], row_send.at[step], row_recv.at[step], at(0, peer(step))
        ).wait_send()
        spread(step).wait_send()


def shards(n_blk, n_group, audio_embed, text_embed):
    rows, depth = audio_embed.shape
    cols = text_embed.shape[0]
    parts, steps = 3, 2
    padded = -(-cols // LANES) * LANES
    vmem = pl.BlockSpec(memory_space=pltpu.VMEM)
    dma = pltpu.SemaphoreType.DMA
    grad_audio, grad_text, loss_rows, loss_cols = pl.pallas_call(
        functools.partial(kernel, n_blk, n_group, parts, steps),
        out_shape=(
            jax.ShapeDtypeStruct((cols, depth), f32),
            jax.ShapeDtypeStruct((cols, depth), f32),
            jax.ShapeDtypeStruct((cols,), f32),
            jax.ShapeDtypeStruct((cols,), f32),
        ),
        in_specs=[vmem, vmem],
        out_specs=(vmem, vmem, vmem, vmem),
        scratch_shapes=[
            pltpu.VMEM((SPAN - 1, cols, depth), f32),
            pltpu.VMEM((rows, depth), bf16),
            pltpu.VMEM((rows, depth), bf16),
            pltpu.VMEM((depth, rows), bf16),
            pltpu.VMEM((depth, rows), bf16),
            pltpu.VMEM((SPAN, depth, cols), bf16),
            pltpu.VMEM((SPAN, depth, cols), bf16),
            pltpu.VMEM((SPAN * cols, rows), f32),
            pltpu.VMEM((SPAN * cols, rows), bf16),
            pltpu.VMEM((SPAN * cols, rows), bf16),
            pltpu.VMEM((rows, depth), f32),
            pltpu.VMEM((n_group, cols, depth), f32),
            pltpu.VMEM((SPAN, cols, depth), f32),
            pltpu.VMEM((2, cols, depth), f32),
            pltpu.VMEM((cols, depth), f32),
            pltpu.VMEM((padded, LANES), f32),
            pltpu.VMEM((SPAN, 8, padded), f32),
            pltpu.VMEM((SPAN, SPAN, 8, padded), f32),
            pltpu.VMEM((n_group, 8, rows), f32),
            pltpu.VMEM((8, rows), f32),
            dma((3, parts)), dma((2, parts)),
            dma((SPAN, SPAN)), dma((SPAN, SPAN)),
            dma((n_group,)), dma((n_group,)),
            dma((2, steps)), dma((3, steps)),
            dma((n_group,)), dma((n_group,)),
        ],
        compiler_params=pltpu.CompilerParams(
            collective_id=0, has_side_effects=True, vmem_limit_bytes=56 * 1024 * 1024
        ),
        name="contrast",
    )(audio_embed, text_embed)
    return logit_scale * grad_audio, ln2 * grad_text, ln2 * loss_rows, ln2 * loss_cols


def solution(mesh):
    return jax.shard_map(
        functools.partial(shards, mesh.shape["blk"], mesh.shape["group"]),
        mesh=mesh,
        in_specs=(P("blk", None), P(("blk", "group"), None)),
        out_specs=(
            P(("blk", "group"), None),
            P(("blk", "group"), None),
            P(("blk", "group")),
            P(("blk", "group")),
        ),
        check_vma=False,
    )
```

```python
import functools
import math

import jax
import jax.numpy as jnp
from jax import lax
from jax.experimental import pallas as pl
from jax.experimental.pallas import tpu as pltpu
from jax.sharding import PartitionSpec as P

SPAN = 3
LANES = 128
MESH = pl.DeviceIdType.MESH

logit_scale = 1.0 / 0.07
log2e = math.log2(math.e)
ln2 = math.log(2.0)
bf16 = jnp.bfloat16
f32 = jnp.float32


def split(value):
    high = value.astype(bf16)
    return high, (value - high.astype(f32)).astype(bf16)


def dot(a, b):
    return jnp.dot(a, b, preferred_element_type=f32)


def dot3(a_high, a_low, b_high, b_low):
    return dot(a_high, b_high) + dot(a_high, b_low) + dot(a_low, b_high)


def merge(first, second):
    highest = jnp.maximum(first[0], second[0])
    return (
        highest,
        first[1] * jnp.exp2(first[0] - highest) + second[1] * jnp.exp2(second[0] - highest),
    )


def kernel(
    n_blk, n_group, parts, steps,
    audio_hbm, text_hbm,
    grad_audio, grad_text, loss_rows, loss_cols,
    window, audio_high, audio_low, turned_high, turned_low,
    text_turned_high, text_turned_low, logits, g_high, g_low,
    audio_part, audio_inbox,
    text_part, inbox, relay,
    audio, text, col_term,
    tall, wide, col_box, row_box, row_stat,
    fwd_send, fwd_recv, stat_send, stat_recv, row_send, row_recv,
    back_send, back_recv, ga_send, ga_recv, load_sem,
):
    rows, depth = audio.shape
    cols = text.shape[0]
    chunk = cols // parts
    strip = cols // steps
    padded = wide.shape[2]
    b = lax.axis_index("blk")
    member = lax.axis_index("group")
    odd = lax.rem(b, 2) == 1
    even = lax.rem(b, 2) == 0

    def at(step, group=None):
        return {
            "blk": lax.rem(b + step + n_blk, n_blk),
            "group": member if group is None else group,
        }

    def peer(step):
        return lax.rem(member + step, n_group)

    barrier = pltpu.get_barrier_semaphore()
    for step in (-2, -1, 1, 2):
        pl.semaphore_signal(barrier, inc=1, device_id=at(step), device_id_type=MESH)
    for step in range(1, n_group):
        pl.semaphore_signal(barrier, inc=1, device_id=at(0, peer(step)), device_id_type=MESH)
    loads = (
        pltpu.make_async_copy(text_hbm, text, load_sem.at[0]),
        pltpu.make_async_copy(audio_hbm, audio, load_sem.at[1]),
    )
    for load in loads:
        load.start()
    loads[0].wait()
    pl.semaphore_wait(barrier, 4 + n_group - 1)

    def piece(c):
        return pl.ds(c * chunk, chunk)

    def remote(src, dst, send, recv, device):
        return pltpu.make_async_remote_copy(
            src_ref=src, dst_ref=dst, send_sem=send, recv_sem=recv,
            device_id=device, device_id_type=MESH,
        )

    def near(c):
        return remote(text.at[piece(c)], window.at[0, piece(c)], fwd_send.at[0, c], fwd_recv.at[0, c], at(-1))

    def far(c):
        return remote(text.at[piece(c)], window.at[1, piece(c)], fwd_send.at[1, c], fwd_recv.at[1, c], at(-2))

    def pass_on(c):
        return remote(
            window.at[0, piece(c)], window.at[1, piece(c)], fwd_send.at[2, c], fwd_recv.at[1, c], at(-1)
        )

    for c in range(parts):
        near(c).start()
    loads[1].wait()
    scaled = audio[...] * (logit_scale * log2e)
    high, low = split(scaled)
    audio_high[...] = high
    audio_low[...] = low
    turned = scaled.T
    high, low = split(turned)
    turned_high[...] = high
    turned_low[...] = low
    tall[...] = jnp.zeros_like(tall)
    row_stat[...] = jnp.zeros_like(row_stat)

    def positive(c):
        ids_text = lax.broadcasted_iota(jnp.int32, (strip, rows), 0)
        ids_audio = lax.broadcasted_iota(jnp.int32, (strip, rows), 1)
        return ids_audio == ids_text + (member * cols + c * strip)

    lane = lax.broadcasted_iota(jnp.int32, (chunk, LANES), 1)

    def stat_copy(mine, theirs):
        return remote(
            wide.at[mine], col_box.at[theirs, mine],
            stat_send.at[theirs, mine], stat_recv.at[theirs, mine], at(mine - theirs),
        )

    for k in range(SPAN):
        if k == 1:
            @pl.when(odd)
            def _():
                far(0).start()

        for c in range(parts):
            if k == 0:
                block = text[piece(c)]
            else:
                if k == 1:
                    near(c).wait_recv()

                    @pl.when(odd)
                    def _():
                        pass_on(c).start()
                        if c + 1 < parts:
                            far(c + 1).start()
                else:
                    far(c).wait_recv()
                block = window[k - 1, piece(c)]
            high, low = split(block)
            start = k * cols + c * chunk
            tile = dot3(high, low, turned_high[...], turned_low[...])
            logits[pl.ds(start, chunk)] = tile
            top = jnp.max(tile, axis=1, keepdims=True)
            total = jnp.sum(jnp.exp2(tile - top), axis=1, keepdims=True)
            tall[piece(c)] = jnp.where(lane == 0, top, total)
            top = jnp.max(tile, axis=0, keepdims=True)
            if start:
                top = jnp.maximum(top, row_stat[0:1])
            total = jnp.sum(jnp.exp2(tile - top), axis=0, keepdims=True)
            if start:
                total = total + row_stat[1:2] * jnp.exp2(row_stat[0:1] - top)
            row_stat[0:1] = top
            row_stat[1:2] = total
        wide[k] = tall[...].T[0:8]
        for theirs in range(SPAN):
            if theirs != k:
                stat_copy(k, theirs).start()
        if k == SPAN - 1:
            for step in range(1, n_group):
                remote(
                    row_stat, row_box.at[step], row_send.at[step], row_recv.at[step], at(0, peer(step))
                ).start()
        block = text[...] if k == 0 else window[k - 1]
        high, low = split(block.T)
        text_turned_high[k] = high
        text_turned_low[k] = low

    def stripe(c):
        return pl.ds(c * strip, strip)

    def back(k, c, onward=True):
        part = text_part.at[k, stripe(c)]
        if k == 2 and onward:
            return remote(part, inbox.at[1, stripe(c)], back_send.at[1, c], back_recv.at[1, c], at(2))
        if k == 2:
            return remote(part, relay.at[stripe(c)], back_send.at[1, c], back_recv.at[2, c], at(1))
        return remote(part, inbox.at[0, stripe(c)], back_send.at[0, c], back_recv.at[0, c], at(1))

    def column_lse(k):
        pair = (wide[k, 0:1], wide[k, 1:2])
        for other in range(SPAN):
            if other != k:
                stat_copy(other, k).wait_recv()
                pair = merge(pair, (col_box[k, other, 0:1], col_box[k, other, 1:2]))
        return jnp.broadcast_to(pair[0] + jnp.log2(pair[1]), (LANES, padded)).T

    def column_part(k, c, col_lse):
        tile = logits[pl.ds(k * cols + c * strip, strip)]
        return jnp.exp2(tile - col_lse[c * strip:(c + 1) * strip, 0:1])

    col_lse = column_lse(2)
    for c in range(steps):
        col_term[stripe(c)] = column_part(2, c, col_lse)

    pair = (row_stat[0:1], row_stat[1:2])
    for step in range(1, n_group):
        remote(
            row_stat, row_box.at[step], row_send.at[step], row_recv.at[step], at(0, peer(step))
        ).wait_recv()
        pair = merge(pair, (row_box[step, 0:1], row_box[step, 1:2]))
    row_lse = pair[0] + jnp.log2(pair[1])

    def weights(k, c, col_lse):
        start = k * cols + c * strip
        tile = logits[pl.ds(start, strip)]
        by_column = col_term[stripe(c)] if k == 2 else column_part(k, c, col_lse)
        weight = 0.5 * (jnp.exp2(tile - row_lse) + by_column)
        if k == 0:
            own_lse = col_lse[c * strip:(c + 1) * strip, 0:1]
            here = positive(c)
            weight = jnp.where(here, weight - 1.0, weight)
            score = jnp.sum(jnp.where(here, tile, 0.0), axis=1, keepdims=True)
            own_row = jnp.sum(jnp.where(here, row_lse, 0.0), axis=1, keepdims=True)
            lanes = lax.broadcasted_iota(jnp.int32, (strip, LANES), 1)
            tall[stripe(c)] = jnp.where(lanes == 0, own_row - score, own_lse - score)
        high, low = split(weight)
        g_high[pl.ds(start, strip)] = high
        g_low[pl.ds(start, strip)] = low

    def text_terms(k, c):
        here = pl.ds(k * cols + c * strip, strip)
        return dot3(g_high[here], g_low[here], audio_high[...], audio_low[...])

    for c in range(steps):
        weights(2, c, col_lse)
        text_part[2, stripe(c)] = text_terms(2, c)

        @pl.when(odd)
        def _():
            back(2, c).start()

        @pl.when(even)
        def _():
            back(2, c, False).start()

    for k in (1, 0):
        col_lse = column_lse(k)
        for c in range(steps):
            weights(k, c, col_lse)

    def audio_terms(lanes):
        total = None
        for k in range(SPAN):
            here = (pl.ds(k * cols, cols), lanes)
            term = dot3(text_turned_high[k], text_turned_low[k], g_high[here], g_low[here])
            total = term if total is None else total + term
        return total.T

    def share(group):
        return pl.ds(pl.multiple_of(group * cols, 8), cols)

    slices = cols // LANES if cols % LANES == 0 else 1
    width = cols // slices

    def spread(step, lot):
        start = peer(step) * cols + lot * width
        return remote(
            audio_part.at[pl.ds(pl.multiple_of(start, 8), width)],
            audio_inbox.at[step, pl.ds(lot * width, width)],
            ga_send.at[step, lot], ga_recv.at[step, lot], at(0, peer(step)),
        )

    aligned = cols % LANES == 0

    def own_share(step, lot):
        start = pl.multiple_of(peer(step) * cols + lot * width, width)
        audio_part[pl.ds(start, width)] = audio_terms(pl.ds(start, width))

    if not aligned:
        audio_part[...] = audio_terms(pl.ds(0, rows))
    for step in range(1, n_group):
        for lot in range(slices):
            if aligned:
                own_share(step, lot)
            spread(step, lot).start()

    for c in range(steps):
        text_part[1, stripe(c)] = text_terms(1, c)

        @pl.when(odd)
        def _():
            back(2, c, False).wait_recv()
            text_part[1, stripe(c)] += relay[stripe(c)]

        back(1, c).start()

    losses = tall[...].T
    loss_rows[...] = losses[0:1, 0:cols].reshape(loss_rows.shape)
    loss_cols[...] = losses[1:2, 0:cols].reshape(loss_cols.shape)

    for c in range(steps):
        text_part[0, stripe(c)] = text_terms(0, c)
    if aligned:
        start = pl.multiple_of(member * cols, cols)
        audio_part[share(member)] = audio_terms(pl.ds(start, cols))

    for lot in range(slices):
        rank = pl.ds(lot * width, width)
        total = audio_part[pl.ds(pl.multiple_of(member * cols + lot * width, 8), width)]
        for step in range(1, n_group):
            spread(step, lot).wait_recv()
            total = total + audio_inbox[step, rank]
        grad_audio[rank] = total

    for c in range(steps):
        back(1, c).wait_recv()
        grad_text[stripe(c)] = text_part[0, stripe(c)] + inbox[0, stripe(c)]

        @pl.when(odd)
        def _():
            back(2, c).wait_recv()
            grad_text[stripe(c)] += inbox[1, stripe(c)]

    for c in range(steps):
        back(2, c).wait_send()
        back(1, c).wait_send()

    for c in range(parts):
        near(c).wait_send()

        @pl.when(odd)
        def _():
            far(c).wait_send()
            pass_on(c).wait_send()

    for mine in range(SPAN):
        for theirs in range(SPAN):
            if mine != theirs:
                stat_copy(mine, theirs).wait_send()
    for step in range(1, n_group):
        remote(
            row_stat, row_box.at[step], row_send.at[step], row_recv.at[step], at(0, peer(step))
        ).wait_send()
        for lot in range(slices):
            spread(step, lot).wait_send()


def shards(n_blk, n_group, audio_embed, text_embed):
    rows, depth = audio_embed.shape
    cols = text_embed.shape[0]
    parts, steps = 3, 2
    padded = -(-cols // LANES) * LANES
    slices = cols // LANES if cols % LANES == 0 else 1
    vmem = pl.BlockSpec(memory_space=pltpu.VMEM)
    dma = pltpu.SemaphoreType.DMA
    grad_audio, grad_text, loss_rows, loss_cols = pl.pallas_call(
        functools.partial(kernel, n_blk, n_group, parts, steps),
        out_shape=(
            jax.ShapeDtypeStruct((cols, depth), f32),
            jax.ShapeDtypeStruct((cols, depth), f32),
            jax.ShapeDtypeStruct((cols,), f32),
            jax.ShapeDtypeStruct((cols,), f32),
        ),
        in_specs=[pl.BlockSpec(memory_space=pltpu.HBM)] * 2,
        out_specs=(vmem, vmem, vmem, vmem),
        scratch_shapes=[
            pltpu.VMEM((SPAN - 1, cols, depth), f32),
            pltpu.VMEM((rows, depth), bf16),
            pltpu.VMEM((rows, depth), bf16),
            pltpu.VMEM((depth, rows), bf16),
            pltpu.VMEM((depth, rows), bf16),
            pltpu.VMEM((SPAN, depth, cols), bf16),
            pltpu.VMEM((SPAN, depth, cols), bf16),
            pltpu.VMEM((SPAN * cols, rows), f32),
            pltpu.VMEM((SPAN * cols, rows), bf16),
            pltpu.VMEM((SPAN * cols, rows), bf16),
            pltpu.VMEM((rows, depth), f32),
            pltpu.VMEM((n_group, cols, depth), f32),
            pltpu.VMEM((SPAN, cols, depth), f32),
            pltpu.VMEM((2, cols, depth), f32),
            pltpu.VMEM((cols, depth), f32),
            pltpu.VMEM((rows, depth), f32),
            pltpu.VMEM((cols, depth), f32),
            pltpu.VMEM((cols, rows), f32),
            pltpu.VMEM((padded, LANES), f32),
            pltpu.VMEM((SPAN, 8, padded), f32),
            pltpu.VMEM((SPAN, SPAN, 8, padded), f32),
            pltpu.VMEM((n_group, 8, rows), f32),
            pltpu.VMEM((8, rows), f32),
            dma((3, parts)), dma((2, parts)),
            dma((SPAN, SPAN)), dma((SPAN, SPAN)),
            dma((n_group,)), dma((n_group,)),
            dma((2, steps)), dma((3, steps)),
            dma((n_group, slices)), dma((n_group, slices)), dma((2,)),
        ],
        compiler_params=pltpu.CompilerParams(
            collective_id=0, has_side_effects=True, vmem_limit_bytes=36 * 1024 * 1024
        ),
        name="contrast",
    )(audio_embed, text_embed)
    return logit_scale * grad_audio, ln2 * grad_text, ln2 * loss_rows, ln2 * loss_cols


def solution(mesh):
    return jax.shard_map(
        functools.partial(shards, mesh.shape["blk"], mesh.shape["group"]),
        mesh=mesh,
        in_specs=(P("blk", None), P(("blk", "group"), None)),
        out_specs=(
            P(("blk", "group"), None),
            P(("blk", "group"), None),
            P(("blk", "group")),
            P(("blk", "group")),
        ),
        check_vma=False,
    )
```

```python
import functools
import math

import jax
import jax.numpy as jnp
from jax import lax
from jax.experimental import pallas as pl
from jax.experimental.pallas import tpu as pltpu
from jax.sharding import PartitionSpec as P

SPAN = 3
LANES = 128
MESH = pl.DeviceIdType.MESH

logit_scale = 1.0 / 0.07
log2e = math.log2(math.e)
ln2 = math.log(2.0)
bf16 = jnp.bfloat16
f32 = jnp.float32


def split(value):
    high = value.astype(bf16)
    return high, (value - high.astype(f32)).astype(bf16)


def dot(a, b):
    return jnp.dot(a, b, preferred_element_type=f32)


def dot3(a_high, a_low, b_high, b_low):
    return dot(a_high, b_high) + dot(a_high, b_low) + dot(a_low, b_high)


def merge(first, second):
    highest = jnp.maximum(first[0], second[0])
    return (
        highest,
        first[1] * jnp.exp2(first[0] - highest) + second[1] * jnp.exp2(second[0] - highest),
    )


def kernel(
    n_blk, n_group, parts, steps,
    audio_hbm, text_hbm,
    grad_audio, grad_text, loss_rows, loss_cols,
    window, audio_high, audio_low, turned_high, turned_low,
    text_turned_high, text_turned_low, logits, g_high, g_low,
    audio_part, audio_inbox,
    text_part, inbox, relay,
    audio, text, col_term,
    tall, wide, col_box, row_box, row_stat,
    fwd_send, fwd_recv, stat_send, stat_recv, row_send, row_recv,
    back_send, back_recv, ga_send, ga_recv, load_sem,
):
    rows, depth = audio.shape
    cols = text.shape[0]
    chunk = cols // parts
    strip = cols // steps
    padded = wide.shape[2]
    b = lax.axis_index("blk")
    member = lax.axis_index("group")
    odd = lax.rem(b, 2) == 1
    even = lax.rem(b, 2) == 0

    def at(step, group=None):
        return {
            "blk": lax.rem(b + step + n_blk, n_blk),
            "group": member if group is None else group,
        }

    def peer(step):
        return lax.rem(member + step, n_group)

    barrier = pltpu.get_barrier_semaphore()
    for step in (-2, -1, 1, 2):
        pl.semaphore_signal(barrier, inc=1, device_id=at(step), device_id_type=MESH)
    for step in range(1, n_group):
        pl.semaphore_signal(barrier, inc=1, device_id=at(0, peer(step)), device_id_type=MESH)
    loads = (
        pltpu.make_async_copy(text_hbm, text, load_sem.at[0]),
        pltpu.make_async_copy(audio_hbm, audio, load_sem.at[1]),
    )
    for load in loads:
        load.start()
    loads[0].wait()
    pl.semaphore_wait(barrier, 4 + n_group - 1)

    def piece(c):
        return pl.ds(c * chunk, chunk)

    def remote(src, dst, send, recv, device):
        return pltpu.make_async_remote_copy(
            src_ref=src, dst_ref=dst, send_sem=send, recv_sem=recv,
            device_id=device, device_id_type=MESH,
        )

    def near(c):
        return remote(text.at[piece(c)], window.at[0, piece(c)], fwd_send.at[0, c], fwd_recv.at[0, c], at(-1))

    def far(c):
        return remote(text.at[piece(c)], window.at[1, piece(c)], fwd_send.at[1, c], fwd_recv.at[1, c], at(-2))

    def pass_on(c):
        return remote(
            window.at[0, piece(c)], window.at[1, piece(c)], fwd_send.at[2, c], fwd_recv.at[1, c], at(-1)
        )

    for c in range(parts):
        near(c).start()
    loads[1].wait()
    scaled = audio[...] * (logit_scale * log2e)
    high, low = split(scaled)
    audio_high[...] = high
    audio_low[...] = low
    turned = scaled.T
    high, low = split(turned)
    turned_high[...] = high
    turned_low[...] = low
    tall[...] = jnp.zeros_like(tall)
    row_stat[...] = jnp.zeros_like(row_stat)

    def positive(c):
        ids_text = lax.broadcasted_iota(jnp.int32, (strip, rows), 0)
        ids_audio = lax.broadcasted_iota(jnp.int32, (strip, rows), 1)
        return ids_audio == ids_text + (member * cols + c * strip)

    lane = lax.broadcasted_iota(jnp.int32, (chunk, LANES), 1)

    def stat_copy(mine, theirs):
        return remote(
            wide.at[mine], col_box.at[theirs, mine],
            stat_send.at[theirs, mine], stat_recv.at[theirs, mine], at(mine - theirs),
        )

    for k in range(SPAN):
        if k == 1:
            @pl.when(odd)
            def _():
                far(0).start()

        for c in range(parts):
            if k == 0:
                block = text[piece(c)]
            else:
                if k == 1:
                    near(c).wait_recv()

                    @pl.when(odd)
                    def _():
                        pass_on(c).start()
                        if c + 1 < parts:
                            far(c + 1).start()
                else:
                    far(c).wait_recv()
                block = window[k - 1, piece(c)]
            high, low = split(block)
            start = k * cols + c * chunk
            tile = dot3(high, low, turned_high[...], turned_low[...])
            logits[pl.ds(start, chunk)] = tile
            top = jnp.max(tile, axis=1, keepdims=True)
            total = jnp.sum(jnp.exp2(tile - top), axis=1, keepdims=True)
            tall[piece(c)] = jnp.where(lane == 0, top, total)
            top = jnp.max(tile, axis=0, keepdims=True)
            if start:
                top = jnp.maximum(top, row_stat[0:1])
            total = jnp.sum(jnp.exp2(tile - top), axis=0, keepdims=True)
            if start:
                total = total + row_stat[1:2] * jnp.exp2(row_stat[0:1] - top)
            row_stat[0:1] = top
            row_stat[1:2] = total
        wide[k] = tall[...].T[0:8]
        for theirs in range(SPAN):
            if theirs != k:
                stat_copy(k, theirs).start()
        if k == SPAN - 1:
            for step in range(1, n_group):
                remote(
                    row_stat, row_box.at[step], row_send.at[step], row_recv.at[step], at(0, peer(step))
                ).start()
        block = text[...] if k == 0 else window[k - 1]
        high, low = split(block.T)
        text_turned_high[k] = high
        text_turned_low[k] = low

    def stripe(c):
        return pl.ds(c * strip, strip)

    def back(k, c, onward=True):
        part = text_part.at[k, stripe(c)]
        if k == 2 and onward:
            return remote(part, inbox.at[1, stripe(c)], back_send.at[1, c], back_recv.at[1, c], at(2))
        if k == 2:
            return remote(part, relay.at[stripe(c)], back_send.at[1, c], back_recv.at[2, c], at(1))
        return remote(part, inbox.at[0, stripe(c)], back_send.at[0, c], back_recv.at[0, c], at(1))

    def column_lse(k):
        pair = (wide[k, 0:1], wide[k, 1:2])
        for other in range(SPAN):
            if other != k:
                stat_copy(other, k).wait_recv()
                pair = merge(pair, (col_box[k, other, 0:1], col_box[k, other, 1:2]))
        return jnp.broadcast_to(pair[0] + jnp.log2(pair[1]), (LANES, padded)).T

    def column_part(k, c, col_lse):
        tile = logits[pl.ds(k * cols + c * strip, strip)]
        return jnp.exp2(tile - col_lse[c * strip:(c + 1) * strip, 0:1])

    col_lse = column_lse(2)
    for c in range(steps):
        col_term[stripe(c)] = column_part(2, c, col_lse)

    pair = (row_stat[0:1], row_stat[1:2])
    for step in range(1, n_group):
        remote(
            row_stat, row_box.at[step], row_send.at[step], row_recv.at[step], at(0, peer(step))
        ).wait_recv()
        pair = merge(pair, (row_box[step, 0:1], row_box[step, 1:2]))
    row_lse = pair[0] + jnp.log2(pair[1])

    def weights(k, c, col_lse):
        start = k * cols + c * strip
        tile = logits[pl.ds(start, strip)]
        by_column = col_term[stripe(c)] if k == 2 else column_part(k, c, col_lse)
        weight = 0.5 * (jnp.exp2(tile - row_lse) + by_column)
        if k == 0:
            own_lse = col_lse[c * strip:(c + 1) * strip, 0:1]
            here = positive(c)
            weight = jnp.where(here, weight - 1.0, weight)
            score = jnp.sum(jnp.where(here, tile, 0.0), axis=1, keepdims=True)
            own_row = jnp.sum(jnp.where(here, row_lse, 0.0), axis=1, keepdims=True)
            lanes = lax.broadcasted_iota(jnp.int32, (strip, LANES), 1)
            tall[stripe(c)] = jnp.where(lanes == 0, own_row - score, own_lse - score)
        high, low = split(weight)
        g_high[pl.ds(start, strip)] = high
        g_low[pl.ds(start, strip)] = low

    def text_terms(k, c):
        here = pl.ds(k * cols + c * strip, strip)
        return dot3(g_high[here], g_low[here], audio_high[...], audio_low[...])

    for c in range(steps):
        weights(2, c, col_lse)
        text_part[2, stripe(c)] = text_terms(2, c)

        @pl.when(odd)
        def _():
            back(2, c).start()

        @pl.when(even)
        def _():
            back(2, c, False).start()

    for k in (1, 0):
        col_lse = column_lse(k)
        for c in range(steps):
            weights(k, c, col_lse)

    def audio_terms(lanes):
        total = None
        for k in range(SPAN):
            here = (pl.ds(k * cols, cols), lanes)
            term = dot3(text_turned_high[k], text_turned_low[k], g_high[here], g_low[here])
            total = term if total is None else total + term
        return total.T

    def share(group):
        return pl.ds(pl.multiple_of(group * cols, 8), cols)

    slices = cols // LANES if cols % LANES == 0 else 1
    width = cols // slices

    def spread(step, lot):
        start = peer(step) * cols + lot * width
        return remote(
            audio_part.at[pl.ds(pl.multiple_of(start, 8), width)],
            audio_inbox.at[step, pl.ds(lot * width, width)],
            ga_send.at[step, lot], ga_recv.at[step, lot], at(0, peer(step)),
        )

    aligned = cols % LANES == 0

    def own_share(step, lot):
        start = pl.multiple_of(peer(step) * cols + lot * width, width)
        audio_part[pl.ds(start, width)] = audio_terms(pl.ds(start, width))

    if not aligned:
        audio_part[...] = audio_terms(pl.ds(0, rows))
    for step in range(1, n_group):
        for lot in range(slices):
            if aligned:
                own_share(step, lot)
            spread(step, lot).start()

    for c in range(steps):
        text_part[1, stripe(c)] = text_terms(1, c)

        @pl.when(odd)
        def _():
            back(2, c, False).wait_recv()
            text_part[1, stripe(c)] += relay[stripe(c)]

        back(1, c).start()

    losses = tall[...].T
    loss_rows[...] = losses[0:1, 0:cols].reshape(loss_rows.shape)
    loss_cols[...] = losses[1:2, 0:cols].reshape(loss_cols.shape)

    for c in range(steps):
        text_part[0, stripe(c)] = text_terms(0, c)
    if aligned:
        start = pl.multiple_of(member * cols, cols)
        audio_part[share(member)] = audio_terms(pl.ds(start, cols))

    for lot in range(slices):
        rank = pl.ds(lot * width, width)
        total = audio_part[pl.ds(pl.multiple_of(member * cols + lot * width, 8), width)]
        for step in range(1, n_group):
            spread(step, lot).wait_recv()
            total = total + audio_inbox[step, rank]
        grad_audio[rank] = total

    for c in range(steps):
        back(1, c).wait_recv()
        grad_text[stripe(c)] = text_part[0, stripe(c)] + inbox[0, stripe(c)]

        @pl.when(odd)
        def _():
            back(2, c).wait_recv()
            grad_text[stripe(c)] += inbox[1, stripe(c)]

    for c in range(steps):
        back(2, c).wait_send()
        back(1, c).wait_send()

    for c in range(parts):
        near(c).wait_send()

        @pl.when(odd)
        def _():
            far(c).wait_send()
            pass_on(c).wait_send()

    for mine in range(SPAN):
        for theirs in range(SPAN):
            if mine != theirs:
                stat_copy(mine, theirs).wait_send()
    for step in range(1, n_group):
        remote(
            row_stat, row_box.at[step], row_send.at[step], row_recv.at[step], at(0, peer(step))
        ).wait_send()
        for lot in range(slices):
            spread(step, lot).wait_send()


def shards(n_blk, n_group, audio_embed, text_embed):
    rows, depth = audio_embed.shape
    cols = text_embed.shape[0]
    parts, steps = 3, 2
    padded = -(-cols // LANES) * LANES
    slices = cols // LANES if cols % LANES == 0 else 1
    vmem = pl.BlockSpec(memory_space=pltpu.VMEM)
    dma = pltpu.SemaphoreType.DMA
    grad_audio, grad_text, loss_rows, loss_cols = pl.pallas_call(
        functools.partial(kernel, n_blk, n_group, parts, steps),
        out_shape=(
            jax.ShapeDtypeStruct((cols, depth), f32),
            jax.ShapeDtypeStruct((cols, depth), f32),
            jax.ShapeDtypeStruct((cols,), f32),
            jax.ShapeDtypeStruct((cols,), f32),
        ),
        in_specs=[pl.BlockSpec(memory_space=pltpu.HBM)] * 2,
        out_specs=(vmem, vmem, vmem, vmem),
        scratch_shapes=[
            pltpu.VMEM((SPAN - 1, cols, depth), f32),
            pltpu.VMEM((rows, depth), bf16),
            pltpu.VMEM((rows, depth), bf16),
            pltpu.VMEM((depth, rows), bf16),
            pltpu.VMEM((depth, rows), bf16),
            pltpu.VMEM((SPAN, depth, cols), bf16),
            pltpu.VMEM((SPAN, depth, cols), bf16),
            pltpu.VMEM((SPAN * cols, rows), f32),
            pltpu.VMEM((SPAN * cols, rows), bf16),
            pltpu.VMEM((SPAN * cols, rows), bf16),
            pltpu.VMEM((rows, depth), f32),
            pltpu.VMEM((n_group, cols, depth), f32),
            pltpu.VMEM((SPAN, cols, depth), f32),
            pltpu.VMEM((2, cols, depth), f32),
            pltpu.VMEM((cols, depth), f32),
            pltpu.VMEM((rows, depth), f32),
            pltpu.VMEM((cols, depth), f32),
            pltpu.VMEM((cols, rows), f32),
            pltpu.VMEM((padded, LANES), f32),
            pltpu.VMEM((SPAN, 8, padded), f32),
            pltpu.VMEM((SPAN, SPAN, 8, padded), f32),
            pltpu.VMEM((n_group, 8, rows), f32),
            pltpu.VMEM((8, rows), f32),
            dma((3, parts)), dma((2, parts)),
            dma((SPAN, SPAN)), dma((SPAN, SPAN)),
            dma((n_group,)), dma((n_group,)),
            dma((2, steps)), dma((3, steps)),
            dma((n_group, slices)), dma((n_group, slices)), dma((2,)),
        ],
        compiler_params=pltpu.CompilerParams(
            collective_id=0, has_side_effects=True, vmem_limit_bytes=53 * 1024 * 1024
        ),
        name="contrast",
    )(audio_embed, text_embed)
    return logit_scale * grad_audio, ln2 * grad_text, ln2 * loss_rows, ln2 * loss_cols


def solution(mesh):
    return jax.shard_map(
        functools.partial(shards, mesh.shape["blk"], mesh.shape["group"]),
        mesh=mesh,
        in_specs=(P("blk", None), P(("blk", "group"), None)),
        out_specs=(
            P(("blk", "group"), None),
            P(("blk", "group"), None),
            P(("blk", "group")),
            P(("blk", "group")),
        ),
        check_vma=False,
    )
```
